512 devices in a mesh: seq: 64 (over z, y), head: 2 (over core), base: 4 (over x).
Axes of the slice: x: 4, y: 4, z: 16, core: 2. Of those that a mesh axis runs over, the one named last changes fastest.
Arguments:
- queries: bfloat16 [8192, 2048], P('seq', 'head'), may hold values from -8 to 8
- key_rows: bfloat16 [8192, 2048], P('seq', 'head'), may hold values from -8 to 8
- values: bfloat16 [8192, 2048], P('seq', 'head'), may hold values from -6 to 6
- cotangent: bfloat16 [8192, 2048], P('seq', 'head'), may hold values from -6 to 6
- reference_set: bfloat16 [3, 64, 2048], P(None, None, 'head'), may hold values from -6 to 6
- sample_ids: int32 [4, 8192], P('base'), may hold values from 0 to 63
- mix_weight: float32 [4], P('base'), may hold values from 0.3 to 1
- global_block: int32 [1], replicated, may hold values from 0 to 127
- random_blocks: int32 [16, 128, 2], P('head'), may hold values from 0 to 127, as said below
Outputs:
- attribution: bfloat16 [8192, 2048], P('seq', ('head', 'base'))
The draws below stay inside these ranges and needn't reach their ends.
Inputs may be any that keep to these rules, and one draw needn't show every extreme that they name: `random_blocks`: for the heads of one index of head, at most 1 random entries of the query blocks of one index of seq fall on the key blocks of any one index of seq, and exactly 1 on some.
All inputs are finite; a program needn't handle non-finite values.
Results may differ from the reference program's by a relative error of at most 0.015.
Values may be sent and summed in bfloat16 or wider, within the bound.
No kernel may reach another device: no remote copies, remote signals or barrier semaphores. Data moves between devices by JAX's collectives and lax.ppermute only.
A program may use at most 64 MiB of HBM per device.

```python
import math
import jax
import jax.numpy as jnp
from jax import lax

HEADS = 16
HEAD_DIM = 128
BLOCK = 64
RAND = 2
BANK = 64
BLOCKS_DEV = 2
NB = 128
TOKENS = 8192
SAMPLES = 4
FEAT = 2048


def draw_key_rows(key, part):
    result = jnp.clip(jax.random.normal(jax.random.fold_in(key, 11), (TOKENS, HEADS * HEAD_DIM), jnp.float32), -6.0, 6.0)
    return result.astype(jnp.bfloat16)


def draw_queries(key, part):
    result = jnp.clip(jax.random.normal(jax.random.fold_in(key, 13), (TOKENS, HEADS * HEAD_DIM), jnp.float32), -6.0, 6.0)
    return result.astype(jnp.bfloat16)


def draw_random_blocks(key, part):
    devices = NB // BLOCKS_DEV
    requests = HEADS * RAND * BLOCKS_DEV
    subkeys = jax.random.split(jax.random.fold_in(key, 31), devices)

    def shuffle_owner(subkey):
        return jax.random.permutation(subkey, devices)
    shuffled = jax.vmap(shuffle_owner)(subkeys)
    owners = shuffled[:, jnp.arange(requests) % devices]
    within = jax.random.randint(jax.random.fold_in(key, 37), (devices, requests), 0, BLOCKS_DEV)
    blocks = (owners * BLOCKS_DEV + within).reshape(devices, HEADS, BLOCKS_DEV, RAND)
    return jnp.transpose(blocks, (1, 0, 2, 3)).reshape(HEADS, NB, RAND).astype(jnp.int32)


def set_ends(values, own_key, smallest, largest):
    shape = values.shape
    index_at = [jax.random.randint(jax.random.fold_in(own_key, axis), (), 0, shape[axis]) for axis in range(len(shape))]
    values = values.at[tuple(index_at)].set(smallest)
    longest = shape.index(max(shape))
    index_at[longest] = (index_at[longest] + 1) % shape[longest]
    return values.at[tuple(index_at)].set(largest)


def block_levels(key, extent, pieces, low, high):
    level = 1.0
    for dim, blocks in pieces:
        heights = jax.random.uniform(jax.random.fold_in(jax.random.fold_in(key, 6), dim), (blocks,), jnp.float32, low / len(pieces), high / len(pieces))
        level = level * jnp.repeat(jnp.exp(heights), extent[dim] // blocks).reshape((-1,) + (1,) * (len(extent) - 1 - dim))
    return level


def normal_values(key, extent, width, reach, pieces=(), held_as=jnp.bfloat16):
    entries = jax.random.normal(key, extent, jnp.float32) * width
    if len(pieces) > 0:
        entries = block_levels(key, extent, pieces, -0.22, 0.18) * entries
    return jnp.clip(entries, min=-reach, max=reach).astype(held_as)


def setup_inputs(seed: int = 0) -> dict:
    key_of = jax.random.split(jax.random.key(seed), 10)
    queries = draw_queries(jax.random.fold_in(key_of[9], 71), 0)
    key_rows = draw_key_rows(jax.random.fold_in(key_of[9], 71), 0)
    values = normal_values(key_of[2], (TOKENS, FEAT), 1.0, 6.0, ((0, 64), (1, 2)))
    cotangent = normal_values(key_of[3], (TOKENS, FEAT), 1.0, 6.0, ((0, 64), (1, 2)))
    reference_set = normal_values(key_of[4], (3, BANK, FEAT), 1.0, 6.0, ((2, 2),))
    sample_ids = set_ends(jax.random.randint(key_of[5], (SAMPLES, TOKENS), 0, BANK), jax.random.fold_in(key_of[5], 1), 0, BANK - 1).astype(jnp.int32)
    mix_weight = jnp.clip(0.3 + 0.7 * jax.random.uniform(key_of[6], (SAMPLES,), jnp.float32) ** block_levels(key_of[6], (SAMPLES,), ((0, 4),), -0.2, 0.2), 0.3, 1.0)
    global_block = jax.random.randint(key_of[7], (1,), 0, NB).astype(jnp.int32)
    random_blocks = draw_random_blocks(jax.random.fold_in(key_of[9], 71), 0)
    return dict(queries=queries, key_rows=key_rows, values=values, cotangent=cotangent, reference_set=reference_set, sample_ids=sample_ids, mix_weight=mix_weight, global_block=global_block, random_blocks=random_blocks)


def live_slots(slot_list, block_total):
    inside = (slot_list >= 0) & (slot_list < block_total)
    slot_count = slot_list.shape[-1]
    earlier = slot_list[..., :, None] == slot_list[..., None, :]
    lower_mask = jnp.arange(slot_count)[:, None] > jnp.arange(slot_count)[None, :]
    repeated = jnp.any(earlier & lower_mask, axis=-1)
    return inside & jnp.logical_not(repeated)

def reference(queries, key_rows, values, cotangent, reference_set, sample_ids, mix_weight, global_block, random_blocks):
    feat_all = queries.shape[1]
    head_count = feat_all // HEAD_DIM
    inv_root = 1.0 / math.sqrt(HEAD_DIM)
    high = lax.Precision.HIGHEST
    q_blocks = queries.reshape(NB, BLOCK, feat_all)
    k_blocks = key_rows.reshape(NB, BLOCK, feat_all)
    v_blocks = values.reshape(NB, BLOCK, feat_all)
    out_blocks = cotangent.reshape(NB, BLOCK, feat_all)
    global_id = global_block[0].astype(jnp.int32)
    head_index = jnp.arange(head_count).astype(jnp.int32)[:, None, None]
    row_index = jnp.arange(BLOCK).astype(jnp.int32)[None, None, :]
    grand = jnp.zeros((NB, BLOCK, feat_all), jnp.float32)
    for sample in range(SAMPLES):
        tok_ids = sample_ids[sample].reshape(NB, BLOCK)
        weight = mix_weight[sample]
        base_q = reference_set[0][tok_ids]
        base_k = reference_set[1][tok_ids]
        base_v = reference_set[2][tok_ids]

        def blend_rows(raw_rows, base_rows):
            lifted = base_rows.astype(jnp.float32)
            return (lifted + weight * (raw_rows.astype(jnp.float32) - lifted)).astype(jnp.bfloat16)
        q_mix = blend_rows(q_blocks, base_q)
        k_mix = blend_rows(k_blocks, base_k)
        v_mix = blend_rows(v_blocks, base_v)

        def visit_block(block_pos, totals):
            block_pos = block_pos.astype(jnp.int32)
            window_list = jnp.stack([block_pos - 1, block_pos, block_pos + 1, global_id]).astype(jnp.int32)
            rand_list = random_blocks[:, block_pos, :].astype(jnp.int32)
            slot_list = jnp.concatenate([jnp.broadcast_to(window_list[None, :], (head_count, 4)), rand_list], axis=1)
            live_mask = live_slots(slot_list, NB)
            clipped = jnp.clip(slot_list, 0, NB - 1).astype(jnp.int32)
            pick_index = (clipped[:, :, None], row_index, head_index)

            def pick(array):
                return array.reshape(NB, BLOCK, head_count, HEAD_DIM)[pick_index].astype(jnp.float32)
            q_heads = q_mix[block_pos].astype(jnp.float32).reshape(BLOCK, head_count, HEAD_DIM)
            k_heads = pick(k_mix).reshape(head_count, 6 * BLOCK, HEAD_DIM)
            v_heads = pick(v_mix).reshape(head_count, 6 * BLOCK, HEAD_DIM)
            out_heads = out_blocks[block_pos].astype(jnp.float32).reshape(BLOCK, head_count, HEAD_DIM)
            key_live = jnp.repeat(live_mask, BLOCK, axis=1)[:, None, :]
            scores = jnp.einsum('qhd,hkd->hqk', q_heads, k_heads, precision=high) * inv_root
            scores = jnp.where(key_live, scores, -1e+30)
            row_peak = lax.optimization_barrier(jnp.max(scores, axis=-1, keepdims=True))
            exponent = jnp.where(key_live, jnp.exp(scores - row_peak), 0.0)
            weights_soft = exponent / lax.optimization_barrier(jnp.sum(exponent, axis=-1, keepdims=True))
            probs_low = weights_soft.astype(jnp.bfloat16).astype(jnp.float32)
            attended = jnp.einsum('hqk,hkd->qhd', probs_low, v_heads, precision=high)
            row_term = lax.optimization_barrier(jnp.sum(out_heads * attended, axis=-1))
            dprobs = jnp.einsum('qhd,hkd->hqk', out_heads, v_heads, precision=high)
            dscores = weights_soft * (dprobs - jnp.transpose(row_term)[:, :, None])
            dscore_low = dscores.astype(jnp.bfloat16).astype(jnp.float32)
            grad_q = jnp.einsum('hqk,hkd->qhd', dscore_low, k_heads, precision=high) * inv_root
            grad_k = jnp.einsum('hqk,qhd->hkd', dscore_low, q_heads, precision=high) * inv_root
            grad_v = jnp.einsum('hqk,qhd->hkd', probs_low, out_heads, precision=high)
            key_offset = pick(k_blocks) - pick(base_k)
            value_offset = pick(v_blocks) - pick(base_v)
            key_term = key_offset * grad_k.reshape(head_count, 6, BLOCK, HEAD_DIM) + value_offset * grad_v.reshape(head_count, 6, BLOCK, HEAD_DIM)
            key_term = key_term * live_mask[:, :, None, None].astype(jnp.float32)
            query_offset = q_blocks[block_pos].astype(jnp.float32) - base_q[block_pos].astype(jnp.float32)
            query_term = query_offset * grad_q.reshape(BLOCK, feat_all)
            totals = totals.reshape(NB, BLOCK, head_count, HEAD_DIM).at[pick_index].add(key_term)
            totals = totals.reshape(NB, BLOCK, feat_all)
            return totals.at[block_pos].add(query_term)
        grand = grand + lax.fori_loop(0, NB, visit_block, jnp.zeros((NB, BLOCK, feat_all), jnp.float32))
    return (grand / SAMPLES).astype(jnp.bfloat16).reshape(TOKENS, feat_all)
```

```python
import functools
import math

import jax
import jax.numpy as jnp
from jax import lax
from jax.experimental import pallas as pl
from jax.experimental.pallas import tpu as pltpu
from jax.sharding import PartitionSpec as P

HEAD_DIM = 128
BLOCK = 64
RAND = 2
BF16 = jnp.bfloat16
F32 = jnp.float32


def matmul(left, right, dims):
    return lax.dot_general(left, right, (dims, ((), ())), preferred_element_type=F32)


def attention_kernel(
    samples,
    heads,
    weight_ref,
    live_ref,
    slot_ids_ref,
    query_ids_ref,
    ref_kv_ref,
    ref_q_ref,
    query_ref,
    key_ref,
    value_ref,
    cot_ref,
    below_ref,
    above_ref,
    glob_ref,
    rand_ref,
    local_ref,
    low_rim_ref,
    high_rim_ref,
    glob_term_ref,
    rand_term_ref,
    raw_ref,
    term_ref,
    query_term_ref,
):
    inv_root = 1.0 / math.sqrt(HEAD_DIM)
    bank = ref_q_ref.shape[0]
    near = 6 * BLOCK
    parts, _, _, part_rows, _ = rand_ref.shape
    rank = lax.broadcasted_iota(jnp.int32, (bank, 10 * BLOCK), 0)
    rank_q = lax.broadcasted_iota(jnp.int32, (bank, 2 * BLOCK), 0)
    for head in range(heads):
        cols = slice(head * HEAD_DIM, (head + 1) * HEAD_DIM)
        for kv in range(2):
            own = (key_ref, value_ref)[kv]
            to = slice(kv * HEAD_DIM, (kv + 1) * HEAD_DIM)
            raw_ref[0:64, to] = below_ref[kv, :, cols]
            raw_ref[64:192, to] = own[:, cols]
            raw_ref[192:256, to] = above_ref[kv, :, cols]
            raw_ref[256:320, to] = glob_ref[head, kv]
            raw_ref[320:384, to] = jnp.zeros((BLOCK, HEAD_DIM), BF16)
            for slot in range(2 * RAND):
                for part in range(parts):
                    start = near + slot * BLOCK + part * part_rows
                    raw_ref[start : start + part_rows, to] = rand_ref[
                        part, head * 2 * RAND + slot, kv
                    ]
        live = jnp.concatenate(
            [
                jnp.broadcast_to(live_ref[head, 0:1], (BLOCK, 8 * BLOCK)),
                jnp.broadcast_to(live_ref[head, 1:2], (BLOCK, 8 * BLOCK)),
            ],
            axis=0,
        )
        cot = cot_ref[:, cols]
        for sample in range(samples):
            weight = weight_ref[sample]
            hot = (rank == slot_ids_ref[sample, head]).astype(F32).astype(BF16)
            base = matmul(hot, ref_kv_ref[head], ((0,), (0,)))
            diff = raw_ref[...].astype(F32) - base
            mix = (base + weight * diff).astype(BF16)
            hot_q = (rank_q == query_ids_ref[sample]).astype(F32).astype(BF16)
            base_q = matmul(hot_q, ref_q_ref[:, cols], ((0,), (0,)))
            diff_q = query_ref[:, cols].astype(F32) - base_q
            q_mix = (base_q + weight * diff_q).astype(BF16)
            k_mix = mix[:, 0:HEAD_DIM]
            v_mix = mix[:, HEAD_DIM:]

            def over_keys(rows, keys):
                return jnp.concatenate(
                    [
                        matmul(rows, keys[0:near], ((1,), (1,))),
                        jnp.concatenate(
                            [
                                matmul(rows[0:64], keys[near : near + 128], ((1,), (1,))),
                                matmul(rows[64:128], keys[near + 128 : near + 256], ((1,), (1,))),
                            ],
                            axis=0,
                        ),
                    ],
                    axis=1,
                )

            def to_rows(weights, keys):
                return matmul(weights[:, 0:near], keys[0:near], ((1,), (0,))) + jnp.concatenate(
                    [
                        matmul(weights[0:64, near:], keys[near : near + 128], ((1,), (0,))),
                        matmul(weights[64:128, near:], keys[near + 128 : near + 256], ((1,), (0,))),
                    ],
                    axis=0,
                )

            def to_keys(weights, rows):
                return jnp.concatenate(
                    [
                        matmul(weights[:, 0:near], rows, ((0,), (0,))),
                        matmul(weights[0:64, near:], rows[0:64], ((0,), (0,))),
                        matmul(weights[64:128, near:], rows[64:128], ((0,), (0,))),
                    ],
                    axis=0,
                )

            scores = jnp.where(live > 0.5, over_keys(q_mix, k_mix) * inv_root, -1e30)
            peak = jnp.max(scores, axis=1, keepdims=True)
            exponent = jnp.where(live > 0.5, jnp.exp(scores - peak), 0.0)
            probs = exponent / jnp.sum(exponent, axis=1, keepdims=True)
            probs_low = probs.astype(BF16)
            attended = to_rows(probs_low, v_mix)
            row_term = jnp.sum(cot.astype(F32) * attended, axis=1, keepdims=True)
            dscore = (probs * (over_keys(cot, v_mix) - row_term)).astype(BF16)
            query_term = diff_q * (to_rows(dscore, k_mix) * inv_root)
            term = diff[:, 0:HEAD_DIM] * (to_keys(dscore, q_mix) * inv_root) + diff[
                :, HEAD_DIM:
            ] * to_keys(probs_low, cot)
            if sample == 0:
                term_ref[...] = term
                query_term_ref[...] = query_term
            else:
                term_ref[...] += term
                query_term_ref[...] += query_term
        low_rim_ref[:, cols] = term_ref[0:64].astype(BF16)
        local_ref[:, cols] = term_ref[64:192] + query_term_ref[...]
        high_rim_ref[:, cols] = term_ref[192:256].astype(BF16)
        glob_term_ref[:, cols] = term_ref[256:320]
        for slot in range(2 * RAND):
            for part in range(parts):
                start = near + slot * BLOCK + part * part_rows
                rand_term_ref[part, head * 2 * RAND + slot] = term_ref[
                    start : start + part_rows
                ].astype(BF16)


def attention(
    weights, live, slot_ids, query_ids, ref_kv, ref_q, query, key, value, cot, below, above, glob, rand
):
    samples = weights.shape[0]
    heads = ref_kv.shape[0]
    parts, slots, _, part_rows, _ = rand.shape
    feat = query.shape[1]
    vmem = pl.BlockSpec(memory_space=pltpu.VMEM)
    return pl.pallas_call(
        functools.partial(attention_kernel, samples, heads),
        out_shape=[
            jax.ShapeDtypeStruct((2 * BLOCK, feat), F32),
            jax.ShapeDtypeStruct((BLOCK, feat), BF16),
            jax.ShapeDtypeStruct((BLOCK, feat), BF16),
            jax.ShapeDtypeStruct((BLOCK, feat), F32),
            jax.ShapeDtypeStruct((parts, slots, part_rows, HEAD_DIM), BF16),
        ],
        in_specs=[pl.BlockSpec(memory_space=pltpu.SMEM)] + [vmem] * 13,
        out_specs=[vmem] * 5,
        scratch_shapes=[
            pltpu.VMEM((10 * BLOCK, 2 * HEAD_DIM), BF16),
            pltpu.VMEM((10 * BLOCK, HEAD_DIM), F32),
            pltpu.VMEM((2 * BLOCK, HEAD_DIM), F32),
        ],
        compiler_params=pltpu.CompilerParams(vmem_limit_bytes=32 * 1024 * 1024),
        cost_estimate=pl.CostEstimate(
            flops=900_000_000, bytes_accessed=2_000_000, transcendentals=600_000
        ),
        name="attention",
    )(weights, live, slot_ids, query_ids, ref_kv, ref_q, query, key, value, cot, below, above, glob, rand)


def live_slots(slot_list, block_total):
    inside = (slot_list >= 0) & (slot_list < block_total)
    slot_count = slot_list.shape[-1]
    earlier = slot_list[..., :, None] == slot_list[..., None, :]
    lower_mask = jnp.arange(slot_count)[:, None] > jnp.arange(slot_count)[None, :]
    repeated = jnp.any(earlier & lower_mask, axis=-1)
    return inside & jnp.logical_not(repeated)


def exchange(array, axis):
    return lax.all_to_all(array, axis, 0, 0, tiled=True)


def swapped(array, axis, bit):
    return lax.ppermute(array, axis, [(i, i ^ bit) for i in range(lax.axis_size(axis))])


def take(array, index):
    return array.at[index].get(mode="promise_in_bounds")


def per_device(
    queries,
    key_rows,
    values,
    cotangent,
    reference_set,
    sample_ids,
    mix_weight,
    global_block,
    random_blocks,
):
    seq_count = lax.axis_size("seq")
    seq_rank = lax.axis_index("seq")
    base_count = lax.axis_size("base")
    base_rank = lax.axis_index("base")
    tok_dev, feat_dev = queries.shape
    per_dev = tok_dev // BLOCK
    head_count = feat_dev // HEAD_DIM
    heads = head_count // base_count
    feat = heads * HEAD_DIM
    block_total = per_dev * seq_count
    requests = head_count * per_dev * RAND
    part_rows = BLOCK // base_count
    bank = reference_set.shape[1]
    bits = [1 << i for i in range(seq_count.bit_length() - 1)]
    global_id = global_block[0]

    table = random_blocks.reshape(head_count, seq_count, per_dev, RAND)
    unit = (table % per_dev) * head_count + jnp.arange(head_count)[:, None, None, None]
    wanted = table // per_dev == seq_rank
    pick = jnp.sum(jnp.where(wanted, unit + 1, 0), axis=(0, 2, 3))
    my_table = lax.dynamic_index_in_dim(table, seq_rank, 1, keepdims=False)
    my_owner = (my_table // per_dev).reshape(requests)

    start = base_rank * part_rows

    def row_part(rows):
        cells = rows.reshape(per_dev, BLOCK, head_count, HEAD_DIM)
        cells = lax.dynamic_slice_in_dim(cells, start, part_rows, axis=1)
        return jnp.transpose(cells, (0, 2, 1, 3)).reshape(
            per_dev * head_count, part_rows, HEAD_DIM
        )

    own_units = jnp.stack([row_part(key_rows), row_part(values)], axis=1)
    outgoing = take(own_units, jnp.maximum(pick - 1, 0))
    incoming = exchange(outgoing, "seq")
    fetched = take(incoming, my_owner)
    rand = exchange(fetched, "base").reshape(
        base_count, heads * per_dev * RAND, 2, part_rows, HEAD_DIM
    )

    tok_ids = sample_ids.astype(F32).reshape(-1, HEAD_DIM)
    note = jnp.concatenate(
        [tok_ids, jnp.broadcast_to(mix_weight[:, None], (8, HEAD_DIM))], axis=0
    )
    others = [swapped(note, "base", bit) for bit in (1, 2, 3)]
    notes = jnp.stack([note] + others)
    weights = notes[:, -1, 0]
    ids = notes[:, 0 : tok_ids.shape[0]].astype(jnp.int32).reshape(base_count, block_total, BLOCK)

    def mine(rows):
        return lax.dynamic_slice_in_dim(rows, base_rank * feat, feat, axis=1)

    query, key, value, cot = (mine(rows) for rows in (queries, key_rows, values, cotangent))
    refs = lax.dynamic_slice_in_dim(reference_set, base_rank * feat, feat, axis=2)
    ref_q = refs[0]
    ref_kv = jnp.transpose(refs[1:].reshape(2, bank, heads, HEAD_DIM), (2, 1, 0, 3)).reshape(
        heads, bank, 2 * HEAD_DIM
    )

    pair = jnp.stack([key, value])
    up = [(i, (i + 1) % seq_count) for i in range(seq_count)]
    down = [((i + 1) % seq_count, i) for i in range(seq_count)]
    below = lax.ppermute(pair[:, tok_dev - BLOCK :], "seq", up)
    above = lax.ppermute(pair[:, 0:BLOCK], "seq", down)

    owner_glob = global_id // per_dev
    glob_own = lax.dynamic_slice_in_dim(pair, (global_id % per_dev) * BLOCK, BLOCK, axis=1)
    glob_rows = jnp.transpose(glob_own.reshape(2, BLOCK, heads, HEAD_DIM), (2, 0, 1, 3)).reshape(
        heads * 2 * BLOCK, HEAD_DIM
    )
    distance = owner_glob ^ seq_rank
    for bit in bits:
        came = swapped(glob_rows, "seq", bit)
        glob_rows = jnp.where(distance & -bit == bit, came, glob_rows)
    glob = glob_rows.reshape(heads, 2, BLOCK, HEAD_DIM)

    my_heads = lax.dynamic_slice_in_dim(my_table, base_rank * heads, heads, axis=0)
    block_pos = seq_rank * per_dev + jnp.arange(per_dev)
    window = jnp.stack(
        [block_pos - 1, block_pos, block_pos + 1, jnp.full((per_dev,), global_id)], axis=1
    )
    slot_list = jnp.concatenate(
        [jnp.broadcast_to(window[None], (heads, per_dev, 4)), my_heads], axis=2
    )
    alive = live_slots(slot_list, block_total).astype(F32)
    none = jnp.zeros((heads, 1), F32)
    first = jnp.concatenate([alive[:, 0, 0:3], none, alive[:, 0, 3:4], none, alive[:, 0, 4:]], 1)
    second = jnp.concatenate([none, alive[:, 1, 0:4], none, alive[:, 1, 4:]], 1)
    live = jnp.repeat(jnp.stack([first, second], axis=1), BLOCK, axis=2)
    wide = jnp.clip(seq_rank * per_dev - 1 + jnp.arange(per_dev + 2), 0, block_total - 1)
    near_blocks = jnp.concatenate([wide, global_block, global_block])
    blocks = jnp.concatenate(
        [
            jnp.broadcast_to(near_blocks[None], (heads, per_dev + 4)),
            my_heads.reshape(heads, per_dev * RAND),
        ],
        axis=1,
    )
    slot_ids = ids.at[:, blocks.reshape(-1)].get(mode="promise_in_bounds").reshape(
        base_count, heads, 1, blocks.shape[1] * BLOCK
    )
    query_ids = lax.dynamic_slice_in_dim(ids, seq_rank * per_dev, per_dev, axis=1).reshape(
        base_count, 1, tok_dev
    )

    local, low_rim, high_rim, glob_term, rand_term = attention(
        weights, live, slot_ids, query_ids, ref_kv, ref_q, query, key, value, cot, below, above, glob, rand
    )

    from_above = lax.ppermute(low_rim, "seq", down)
    from_below = lax.ppermute(high_rim, "seq", up)

    for bit in bits:
        glob_term = glob_term + swapped(glob_term.astype(BF16), "seq", bit).astype(F32)

    terms = exchange(rand_term.reshape(-1, part_rows, HEAD_DIM), "base")
    order = jnp.arange(1, requests + 1)
    sent = jnp.sum(
        jnp.where(my_owner[None, :] == jnp.arange(seq_count)[:, None], order[None, :], 0), axis=1
    )
    arrived = exchange(take(terms, jnp.maximum(sent - 1, 0)), "seq")
    units = per_dev * head_count
    place = (pick[None, :] == jnp.arange(1, units + 1)[:, None]).astype(BF16)
    back = matmul(place, arrived, ((1,), (0,)))
    back = jnp.transpose(
        back.astype(BF16).reshape(per_dev, base_count, heads, part_rows, HEAD_DIM), (1, 0, 2, 3, 4)
    )
    back = exchange(back.reshape(-1, part_rows, HEAD_DIM), "base").reshape(
        base_count, per_dev, heads, part_rows, HEAD_DIM
    )
    back = jnp.transpose(back, (1, 0, 3, 2, 4)).reshape(tok_dev, feat).astype(F32)
    glob_rows_total = glob_term
    is_place = (jnp.arange(per_dev) + seq_rank * per_dev == global_id).astype(F32)
    glob_add = (is_place[:, None, None] * glob_rows_total[None]).reshape(tok_dev, feat)
    edges = jnp.concatenate([from_below, from_above], axis=0).astype(F32)
    total = local + edges + glob_add + back
    return (total / base_count).astype(BF16)


def solution(mesh):
    placed = (
        P("seq", "head"),
        P("seq", "head"),
        P("seq", "head"),
        P("seq", "head"),
        P(None, None, "head"),
        P("base", None),
        P("base"),
        P(),
        P("head", None, None),
    )
    return jax.shard_map(
        per_device,
        mesh=mesh,
        in_specs=placed,
        out_specs=P("seq", ("head", "base")),
        check_vma=False,
    )
```

```python
import functools
import math

import jax
import jax.numpy as jnp
from jax import lax
from jax.experimental import pallas as pl
from jax.experimental.pallas import tpu as pltpu
from jax.sharding import PartitionSpec as P

HEAD_DIM = 128
BLOCK = 64
RAND = 2
SEQ_MINOR = 4
PIECE = 8
NOTE_ROWS = 16
NEAR = 6 * BLOCK
BF16 = jnp.bfloat16
F32 = jnp.float32
VMEM = pl.BlockSpec(memory_space=pltpu.VMEM)
SMEM = pl.BlockSpec(memory_space=pltpu.SMEM)


def matmul(left, right, dims):
    return lax.dot_general(left, right, (dims, ((), ())), preferred_element_type=F32)


def columns(first):
    return pl.ds(pl.multiple_of(first, HEAD_DIM), HEAD_DIM)


def prepare_kernel(
    part_rows, heads, glob_ref, pick_ref, key_ref, value_ref, outgoing_ref, low_ref, high_ref
):
    base_rank = lax.axis_index("base")
    head_count = key_ref.shape[1] // HEAD_DIM
    glob_start = pl.multiple_of((glob_ref[0] % 2) * BLOCK, BLOCK)
    for slot in range(pick_ref.shape[0]):
        unit = jnp.maximum(pick_ref[slot] - 1, 0)
        rows = pl.ds(
            pl.multiple_of((unit // head_count) * BLOCK + base_rank * part_rows, part_rows),
            part_rows,
        )
        cols = columns((unit % head_count) * HEAD_DIM)
        outgoing_ref[slot, 0:part_rows] = key_ref[rows, cols]
        outgoing_ref[slot, part_rows : 2 * part_rows] = value_ref[rows, cols]
    pieces = heads * 2 * BLOCK // PIECE
    for head in range(heads):
        cols = columns((base_rank * heads + head) * HEAD_DIM)
        for kv in range(2):
            own = (key_ref, value_ref)[kv]
            unit = slice((head * 2 + kv) * BLOCK, (head * 2 + kv + 1) * BLOCK)
            low_ref[unit] = own[0:BLOCK, cols]
            high_ref[unit] = own[BLOCK:, cols]
            rows = own[pl.ds(glob_start, BLOCK), cols].astype(F32)
            for i in range(BLOCK // PIECE):
                piece = rows[i * PIECE : (i + 1) * PIECE].astype(BF16)
                first = (head * 2 + kv) * (BLOCK // PIECE) + i
                for slot in range(first, pick_ref.shape[0], pieces):
                    outgoing_ref[slot, 2 * part_rows :] = piece


def prepare(glob_block, pick, key_rows, value_rows, part_rows, heads):
    edge = jax.ShapeDtypeStruct((heads * 2 * BLOCK, HEAD_DIM), BF16)
    return pl.pallas_call(
        functools.partial(prepare_kernel, part_rows, heads),
        out_shape=[
            jax.ShapeDtypeStruct((pick.shape[0], 2 * part_rows + PIECE, HEAD_DIM), BF16),
            edge,
            edge,
        ],
        in_specs=[SMEM, SMEM, VMEM, VMEM],
        out_specs=[VMEM] * 3,
        cost_estimate=pl.CostEstimate(flops=0, bytes_accessed=1_400_000, transcendentals=0),
        name="prepare",
    )(glob_block, pick, key_rows, value_rows)


def gather_kernel(
    part_rows, block_total, place_ref, table_ref, weight_ref, ids_ref, incoming_ref, *out_refs
):
    requests = table_ref.shape[0] // len(out_refs)
    lane = lax.broadcasted_iota(jnp.int32, (1, HEAD_DIM), 1)

    def block_row(block, half):
        row = ids_ref[pl.ds(block // 2, 1), :]
        return jnp.where(block % 2 == half, row, pltpu.roll(row, BLOCK, 1))

    def pair_row(left, right):
        return jnp.where(lane < BLOCK, block_row(left, 0), block_row(right, 1))

    first = place_ref[0] * 2
    glob = place_ref[2]
    below = jnp.maximum(first - 1, 0)
    above = jnp.minimum(first + 2, block_total - 1)
    shared = [pair_row(below, first), pair_row(first + 1, above), pair_row(glob, glob)]
    own = [pair_row(first, first + 1)]
    weight = jnp.full((1, HEAD_DIM), weight_ref[0], F32)
    high = weight.astype(BF16).astype(F32)
    rest = weight - high
    middle = rest.astype(BF16).astype(F32)
    pieces = jnp.where(lane == 0, high, jnp.where(lane == 1, middle, rest - middle))
    blank = jnp.zeros((NOTE_ROWS - 5 - requests // 2, HEAD_DIM), F32)
    for step, out_ref in enumerate(out_refs):
        base = place_ref[1] ^ step
        for request in range(requests):
            owner = table_ref[base * requests + request] // 2
            out_ref[request * 2 * part_rows : (request + 1) * 2 * part_rows] = incoming_ref[
                owner, 0 : 2 * part_rows
            ]
        drawn = [
            pair_row(table_ref[base * requests + 2 * i], table_ref[base * requests + 2 * i + 1])
            for i in range(requests // 2)
        ]
        notes = jnp.concatenate(
            [row.astype(F32) for row in shared + own + drawn] + [pieces, blank], axis=0
        )
        out_ref[requests * 2 * part_rows :] = notes.astype(BF16)


def gather(place, table, weight, ids, incoming, bases, part_rows, block_total):
    rows = table.shape[0] // bases * 2 * part_rows + NOTE_ROWS
    return pl.pallas_call(
        functools.partial(gather_kernel, part_rows, block_total),
        out_shape=[jax.ShapeDtypeStruct((rows, HEAD_DIM), BF16)] * bases,
        in_specs=[SMEM, SMEM, SMEM, VMEM, VMEM],
        out_specs=[VMEM] * bases,
        cost_estimate=pl.CostEstimate(flops=0, bytes_accessed=1_000_000, transcendentals=0),
        name="gather",
    )(place, table, weight, ids, incoming)


def attention_kernel(
    samples,
    heads,
    part_rows,
    block_total,
    place_ref,
    table_ref,
    refs_ref,
    query_ref,
    key_ref,
    value_ref,
    cot_ref,
    glob_ref,
    below_ref,
    above_ref,
    *refs,
):
    rand_refs = refs[0:samples]
    (
        local_ref,
        glob_term_ref,
        low_rim_ref,
        high_rim_ref,
        rand_term_ref,
        raw_ref,
        term_ref,
        query_term_ref,
    ) = refs[samples:]
    inv_root = 1.0 / math.sqrt(HEAD_DIM)
    bank = refs_ref.shape[1]
    parts = samples
    slots = 2 * RAND
    seq_rank, base_rank, glob_block = place_ref[0], place_ref[1], place_ref[2]
    rank = lax.broadcasted_iota(jnp.int32, (bank, HEAD_DIM), 0).astype(F32)
    lane = lax.broadcasted_iota(jnp.int32, (BLOCK, HEAD_DIM), 1)
    note_start = rand_refs[0].shape[0] - NOTE_ROWS
    own_notes = 3
    drawn_notes = 4
    weight_note = drawn_notes + heads * RAND
    for head in range(heads):
        first_col = (base_rank * heads + head) * HEAD_DIM
        cols = columns(first_col)
        here = slice(head * HEAD_DIM, (head + 1) * HEAD_DIM)
        for kv in range(2):
            own = (key_ref, value_ref)[kv]
            to = slice(kv * HEAD_DIM, (kv + 1) * HEAD_DIM)
            unit = slice((head * 2 + kv) * BLOCK, (head * 2 + kv + 1) * BLOCK)
            raw_ref[0:64, to] = below_ref[unit]
            raw_ref[64:192, to] = own[:, cols]
            raw_ref[192:256, to] = above_ref[unit]
            raw_ref[256:320, to] = glob_ref[unit]
            raw_ref[320:384, to] = jnp.zeros((BLOCK, HEAD_DIM), BF16)
            for slot in range(slots):
                for step in range(parts):
                    start = NEAR + slot * BLOCK + (base_rank ^ step) * part_rows
                    source = ((head * slots + slot) * 2 + kv) * part_rows
                    raw_ref[pl.ds(pl.multiple_of(start, part_rows), part_rows), to] = rand_refs[
                        step
                    ][source : source + part_rows]

        def live_rows(index):
            here_block = seq_rank * 2 + index
            listed = [here_block - 1, here_block, here_block + 1, glob_block]
            for slot in range(RAND):
                listed.append(table_ref[((base_rank * heads + head) * 2 + index) * RAND + slot])
            alive = []
            for slot, block in enumerate(listed):
                flag = (block >= 0) & (block < block_total)
                for earlier in listed[:slot]:
                    flag = flag & (block != earlier)
                alive.append(jnp.where(flag, 1.0, 0.0))
            dead = jnp.float32(0.0)
            window = [dead] * index + alive[0:3] + [dead] * (1 - index)
            ordered = window + [alive[3], dead] + alive[4:]
            return jnp.concatenate(
                [
                    jnp.where(lane < BLOCK, ordered[2 * i], ordered[2 * i + 1])
                    for i in range(len(ordered) // 2)
                ],
                axis=1,
            )

        live = jnp.concatenate([live_rows(0), live_rows(1)], axis=0) > 0.5
        cot = cot_ref[:, cols]
        ref_q = refs_ref[0, :, cols]
        ref_kv = jnp.concatenate([refs_ref[1, :, cols], refs_ref[2, :, cols]], axis=1)
        query = query_ref[:, cols].astype(F32)
        for sample in range(samples):
            notes = rand_refs[sample][note_start:].astype(F32)
            drawn = drawn_notes + head * RAND

            def hot(row):
                return jnp.where(rank == notes[row : row + 1], 1.0, 0.0).astype(BF16)

            weight = (
                notes[weight_note : weight_note + 1, 0:1]
                + notes[weight_note : weight_note + 1, 1:2]
                + notes[weight_note : weight_note + 1, 2:3]
            )
            hot_keys = jnp.concatenate([hot(0), hot(1), hot(2), hot(drawn), hot(drawn + 1)], axis=1)
            base = matmul(hot_keys, ref_kv, ((0,), (0,)))
            diff = raw_ref[...].astype(F32) - base
            mix = (base + weight * diff).astype(BF16)
            base_q = matmul(hot(own_notes), ref_q, ((0,), (0,)))
            diff_q = query - base_q
            q_mix = (base_q + weight * diff_q).astype(BF16)
            k_mix = mix[:, 0:HEAD_DIM]
            v_mix = mix[:, HEAD_DIM:]

            def over_keys(rows, keys):
                return jnp.concatenate(
                    [
                        matmul(rows, keys[0:NEAR], ((1,), (1,))),
                        jnp.concatenate(
                            [
                                matmul(rows[0:64], keys[NEAR : NEAR + 128], ((1,), (1,))),
                                matmul(rows[64:128], keys[NEAR + 128 : NEAR + 256], ((1,), (1,))),
                            ],
                            axis=0,
                        ),
                    ],
                    axis=1,
                )

            def to_rows(weights, keys):
                return matmul(weights[:, 0:NEAR], keys[0:NEAR], ((1,), (0,))) + jnp.concatenate(
                    [
                        matmul(weights[0:64, NEAR:], keys[NEAR : NEAR + 128], ((1,), (0,))),
                        matmul(weights[64:128, NEAR:], keys[NEAR + 128 : NEAR + 256], ((1,), (0,))),
                    ],
                    axis=0,
                )

            def to_keys(weights, rows):
                return jnp.concatenate(
                    [
                        matmul(weights[:, 0:NEAR], rows, ((0,), (0,))),
                        matmul(weights[0:64, NEAR:], rows[0:64], ((0,), (0,))),
                        matmul(weights[64:128, NEAR:], rows[64:128], ((0,), (0,))),
                    ],
                    axis=0,
                )

            scores = jnp.where(live, over_keys(q_mix, k_mix) * inv_root, -1e30)
            peak = jnp.max(scores, axis=1, keepdims=True)
            exponent = jnp.where(live, jnp.exp(scores - peak), 0.0)
            probs = exponent / jnp.sum(exponent, axis=1, keepdims=True)
            probs_low = probs.astype(BF16)
            attended = to_rows(probs_low, v_mix)
            row_term = jnp.sum(cot.astype(F32) * attended, axis=1, keepdims=True)
            dscore = (probs * (over_keys(cot, v_mix) - row_term)).astype(BF16)
            query_term = diff_q * (to_rows(dscore, k_mix) * inv_root)
            term = diff[:, 0:HEAD_DIM] * (to_keys(dscore, q_mix) * inv_root) + diff[
                :, HEAD_DIM:
            ] * to_keys(probs_low, cot)
            if sample == 0:
                term_ref[...] = term
                query_term_ref[...] = query_term
            else:
                term_ref[...] += term
                query_term_ref[...] += query_term
        low_rim_ref[:, here] = term_ref[0:64].astype(BF16)
        high_rim_ref[:, here] = term_ref[192:256].astype(BF16)
        local_ref[:, here] = term_ref[64:192] + query_term_ref[...]
        glob_term_ref[head * BLOCK : (head + 1) * BLOCK] = term_ref[256:320].astype(BF16)
        for slot in range(slots):
            for part in range(parts):
                start = NEAR + slot * BLOCK + part * part_rows
                rand_term_ref[part, head * slots + slot] = term_ref[
                    start : start + part_rows
                ].astype(BF16)


def attention(
    place, table, refs, query, key, value, cot, glob, below, above, rand, part_rows, heads, block_total
):
    samples = len(rand)
    slots = heads * 2 * RAND
    feat = heads * HEAD_DIM
    return pl.pallas_call(
        functools.partial(attention_kernel, samples, heads, part_rows, block_total),
        out_shape=[
            jax.ShapeDtypeStruct((2 * BLOCK, feat), F32),
            jax.ShapeDtypeStruct((heads * BLOCK, HEAD_DIM), BF16),
            jax.ShapeDtypeStruct((BLOCK, feat), BF16),
            jax.ShapeDtypeStruct((BLOCK, feat), BF16),
            jax.ShapeDtypeStruct((samples, slots, part_rows, HEAD_DIM), BF16),
        ],
        in_specs=[SMEM, SMEM] + [VMEM] * (8 + samples),
        out_specs=[VMEM] * 5,
        scratch_shapes=[
            pltpu.VMEM((10 * BLOCK, 2 * HEAD_DIM), BF16),
            pltpu.VMEM((10 * BLOCK, HEAD_DIM), F32),
            pltpu.VMEM((2 * BLOCK, HEAD_DIM), F32),
        ],
        compiler_params=pltpu.CompilerParams(vmem_limit_bytes=32 * 1024 * 1024),
        cost_estimate=pl.CostEstimate(
            flops=900_000_000, bytes_accessed=2_000_000, transcendentals=600_000
        ),
        name="attention",
    )(place, table, refs, query, key, value, cot, glob, below, above, *rand)


def collect_kernel(heads, place_ref, pick_ref, arrived_ref, *refs):
    out_refs, sum_ref, total_ref = refs[0:-2], refs[-2], refs[-1]
    bases = len(out_refs)
    part_rows = total_ref.shape[1]
    head_count = heads * bases
    total_ref[...] = jnp.zeros_like(total_ref)
    glob = arrived_ref[0, part_rows:].astype(F32)
    for slot in range(pick_ref.shape[0]):
        unit = pick_ref[slot]
        total_ref[unit] += arrived_ref[slot, 0:part_rows].astype(F32)
        if slot:
            glob = glob + arrived_ref[slot, part_rows:].astype(F32)
    for copy in range(sum_ref.shape[0]):
        sum_ref[copy] = glob.astype(BF16)
    for step, out_ref in enumerate(out_refs):
        base = place_ref[1] ^ step
        for block in range(2):
            for head in range(heads):
                out_ref[block * heads + head] = total_ref[
                    1 + block * head_count + base * heads + head
                ].astype(BF16)


def collect(place, pick, arrived, bases, part_rows, heads, copies):
    rows = arrived.shape[1] - part_rows
    return pl.pallas_call(
        functools.partial(collect_kernel, heads),
        out_shape=[jax.ShapeDtypeStruct((2 * heads, part_rows, HEAD_DIM), BF16)] * bases
        + [jax.ShapeDtypeStruct((copies, rows, HEAD_DIM), BF16)],
        in_specs=[SMEM, SMEM, VMEM],
        out_specs=[VMEM] * (bases + 1),
        scratch_shapes=[pltpu.VMEM((1 + 2 * heads * bases, part_rows, HEAD_DIM), F32)],
        cost_estimate=pl.CostEstimate(flops=0, bytes_accessed=500_000, transcendentals=0),
        name="collect",
    )(place, pick, arrived)


def finish_kernel(heads, place_ref, local_ref, low_ref, high_ref, glob_ref, *refs):
    back_refs, out_ref, total_ref = refs[0:-2], refs[-2], refs[-1]
    bases = len(back_refs)
    part_rows = back_refs[0].shape[1]
    total_ref[0:BLOCK] = local_ref[0:BLOCK] + low_ref[...].astype(F32)
    total_ref[BLOCK:] = local_ref[BLOCK:] + high_ref[...].astype(F32)
    for head in range(heads):
        here = slice(head * HEAD_DIM, (head + 1) * HEAD_DIM)
        for step, back_ref in enumerate(back_refs):
            for block in range(2):
                start = block * BLOCK + (place_ref[1] ^ step) * part_rows
                rows = pl.ds(pl.multiple_of(start, part_rows), part_rows)
                total_ref[rows, here] += back_ref[block * heads + head].astype(F32)
        glob = glob_ref[head * BLOCK : (head + 1) * BLOCK].astype(F32)
        for block in range(2):
            rows = slice(block * BLOCK, (block + 1) * BLOCK)
            mine = place_ref[0] * 2 + block == place_ref[2]
            total_ref[rows, here] += jnp.where(mine, glob, 0.0)
    out_ref[...] = (total_ref[...] * (1.0 / bases)).astype(BF16)


def finish(place, local, low, high, glob, back, heads):
    return pl.pallas_call(
        functools.partial(finish_kernel, heads),
        out_shape=jax.ShapeDtypeStruct(local.shape, BF16),
        in_specs=[SMEM] + [VMEM] * (4 + len(back)),
        out_specs=VMEM,
        scratch_shapes=[pltpu.VMEM(local.shape, F32)],
        cost_estimate=pl.CostEstimate(flops=0, bytes_accessed=400_000, transcendentals=0),
        name="finish",
    )(place, local, low, high, glob, *back)


def exchange(array, axis, groups=None):
    return lax.all_to_all(array, axis, 0, 0, axis_index_groups=groups, tiled=True)


def swapped(arrays):
    return [arrays[0]] + [
        lax.ppermute(arrays[step], "base", [(i, i ^ step) for i in range(len(arrays))])
        for step in range(1, len(arrays))
    ]


def take(array, index):
    return array.at[index].get(mode="promise_in_bounds")


def per_device(
    queries,
    key_rows,
    values,
    cotangent,
    reference_set,
    sample_ids,
    mix_weight,
    global_block,
    random_blocks,
):
    seq_count = lax.axis_size("seq")
    seq_rank = lax.axis_index("seq")
    base_count = lax.axis_size("base")
    base_rank = lax.axis_index("base")
    tok_dev, feat_dev = queries.shape
    per_dev = tok_dev // BLOCK
    head_count = feat_dev // HEAD_DIM
    heads = head_count // base_count
    feat = heads * HEAD_DIM
    block_total = per_dev * seq_count
    requests = head_count * per_dev * RAND
    part_rows = BLOCK // base_count
    global_id = global_block[0]
    owner_glob = global_id // per_dev
    place = jnp.stack([seq_rank, base_rank, global_id]).astype(jnp.int32)

    table = random_blocks.reshape(head_count, seq_count, per_dev, RAND)
    unit = (table % per_dev) * head_count + jnp.arange(head_count)[:, None, None, None]
    wanted = table // per_dev == seq_rank
    pick = jnp.sum(jnp.where(wanted, unit + 1, 0), axis=(0, 2, 3))
    my_table = lax.dynamic_index_in_dim(table, seq_rank, 1, keepdims=False).reshape(requests)
    my_owner = my_table // per_dev

    outgoing, low, high = prepare(global_block, pick, key_rows, values, part_rows, heads)

    up = [(i, (i + 1) % seq_count) for i in range(seq_count)]
    down = [((i + 1) % seq_count, i) for i in range(seq_count)]
    below = lax.ppermute(high, "seq", up)
    above = lax.ppermute(low, "seq", down)

    incoming = exchange(outgoing, "seq")
    piece = lax.dynamic_index_in_dim(incoming, owner_glob, 0, keepdims=False)[2 * part_rows :]
    glob = exchange(jnp.broadcast_to(piece[None], (seq_count,) + piece.shape), "seq")
    glob = glob[0 : low.shape[0] // PIECE].reshape(low.shape)
    ids = sample_ids.reshape(-1, HEAD_DIM)
    rand = swapped(
        gather(place, my_table, mix_weight, ids, incoming, base_count, part_rows, block_total)
    )

    local, glob_term, low_rim, high_rim, rand_term = attention(
        place,
        my_table,
        reference_set,
        queries,
        key_rows,
        values,
        cotangent,
        glob,
        below,
        above,
        rand,
        part_rows,
        heads,
        block_total,
    )

    from_above = lax.ppermute(low_rim, "seq", down)
    from_below = lax.ppermute(high_rim, "seq", up)

    terms = exchange(rand_term.reshape(-1, part_rows, HEAD_DIM), "base")
    order = jnp.arange(1, requests + 1)
    sent = jnp.sum(
        jnp.where(my_owner[None, :] == jnp.arange(seq_count)[:, None], order[None, :], 0), axis=1
    )
    major = seq_count // SEQ_MINOR
    shares = jnp.repeat(glob_term.reshape(major, -1, HEAD_DIM), SEQ_MINOR, axis=0)
    returning = jnp.concatenate([take(terms, jnp.maximum(sent - 1, 0)), shares], axis=1)
    arrived = exchange(returning, "seq")
    arrived, from_below, from_above = lax.optimization_barrier((arrived, from_below, from_above))
    *back, share = collect(place, pick, arrived, base_count, part_rows, heads, major)
    back = swapped(back)
    lines = [[i * SEQ_MINOR + j for i in range(major)] for j in range(SEQ_MINOR)]
    glob_total = exchange(share, "seq", lines).reshape(glob_term.shape)
    return finish(place, local, from_below, from_above, glob_total, back, heads)


def solution(mesh):
    placed = (
        P("seq", "head"),
        P("seq", "head"),
        P("seq", "head"),
        P("seq", "head"),
        P(None, None, "head"),
        P("base", None),
        P("base"),
        P(),
        P("head", None, None),
    )
    return jax.shard_map(
        per_device,
        mesh=mesh,
        in_specs=placed,
        out_specs=P("seq", ("head", "base")),
        check_vma=False,
    )
```

```python
import functools
import math

import jax
import jax.numpy as jnp
from jax import lax
from jax.experimental import pallas as pl
from jax.experimental.pallas import tpu as pltpu
from jax.sharding import PartitionSpec as P

HEAD_DIM = 128
BLOCK = 64
RAND = 2
SHARES = 16
PIECE = 8
NOTE_ROWS = 16
NEAR = 6 * BLOCK
BF16 = jnp.bfloat16
F32 = jnp.float32
VMEM = pl.BlockSpec(memory_space=pltpu.VMEM)
SMEM = pl.BlockSpec(memory_space=pltpu.SMEM)


def matmul(left, right, dims):
    return lax.dot_general(left, right, (dims, ((), ())), preferred_element_type=F32)


def columns(first):
    return pl.ds(pl.multiple_of(first, HEAD_DIM), HEAD_DIM)


def prepare_kernel(
    part_rows, heads, glob_ref, pick_ref, key_ref, value_ref, outgoing_ref, low_ref, high_ref
):
    base_rank = lax.axis_index("base")
    head_count = key_ref.shape[1] // HEAD_DIM
    glob_start = pl.multiple_of((glob_ref[0] % 2) * BLOCK, BLOCK)

    def one_slot(slot, carry):
        unit = jnp.maximum(pick_ref[slot] - 1, 0)
        rows = pl.ds(
            pl.multiple_of((unit // head_count) * BLOCK + base_rank * part_rows, part_rows),
            part_rows,
        )
        cols = columns((unit % head_count) * HEAD_DIM)
        outgoing_ref[slot, 0:part_rows] = key_ref[rows, cols]
        outgoing_ref[slot, part_rows : 2 * part_rows] = value_ref[rows, cols]
        return carry

    lax.fori_loop(0, pick_ref.shape[0], one_slot, 0, unroll=8)
    pieces = heads * 2 * BLOCK // PIECE
    for head in range(heads):
        cols = columns((base_rank * heads + head) * HEAD_DIM)
        for kv in range(2):
            own = (key_ref, value_ref)[kv]
            unit = slice((head * 2 + kv) * BLOCK, (head * 2 + kv + 1) * BLOCK)
            low_ref[unit] = own[0:BLOCK, cols]
            high_ref[unit] = own[BLOCK:, cols]
            rows = own[pl.ds(glob_start, BLOCK), cols].astype(F32)
            for i in range(BLOCK // PIECE):
                piece = rows[i * PIECE : (i + 1) * PIECE].astype(BF16)
                first = (head * 2 + kv) * (BLOCK // PIECE) + i
                for slot in range(first, pick_ref.shape[0], pieces):
                    outgoing_ref[slot, 2 * part_rows :] = piece


def prepare(glob_block, pick, key_rows, value_rows, part_rows, heads):
    edge = jax.ShapeDtypeStruct((heads * 2 * BLOCK, HEAD_DIM), BF16)
    return pl.pallas_call(
        functools.partial(prepare_kernel, part_rows, heads),
        out_shape=[
            jax.ShapeDtypeStruct((pick.shape[0], 2 * part_rows + PIECE, HEAD_DIM), BF16),
            edge,
            edge,
        ],
        in_specs=[SMEM, SMEM, VMEM, VMEM],
        out_specs=[VMEM] * 3,
        cost_estimate=pl.CostEstimate(flops=0, bytes_accessed=1_400_000, transcendentals=0),
        name="prepare",
    )(glob_block, pick, key_rows, value_rows)


def gather_kernel(
    part_rows, block_total, place_ref, table_ref, weight_ref, ids_ref, incoming_ref, *out_refs
):
    requests = table_ref.shape[0] // len(out_refs)
    lane = lax.broadcasted_iota(jnp.int32, (1, HEAD_DIM), 1)

    def block_row(block, half):
        row = ids_ref[pl.ds(block // 2, 1), :]
        return jnp.where(block % 2 == half, row, pltpu.roll(row, BLOCK, 1))

    def pair_row(left, right):
        return jnp.where(lane < BLOCK, block_row(left, 0), block_row(right, 1))

    first = place_ref[0] * 2
    glob = place_ref[2]
    below = jnp.maximum(first - 1, 0)
    above = jnp.minimum(first + 2, block_total - 1)
    shared = [pair_row(below, first), pair_row(first + 1, above), pair_row(glob, glob)]
    own = [pair_row(first, first + 1)]
    weight = jnp.full((1, HEAD_DIM), weight_ref[0], F32)
    high = weight.astype(BF16).astype(F32)
    rest = weight - high
    middle = rest.astype(BF16).astype(F32)
    pieces = jnp.where(lane == 0, high, jnp.where(lane == 1, middle, rest - middle))
    blank = jnp.zeros((NOTE_ROWS - 5 - requests // 2, HEAD_DIM), F32)
    for step, out_ref in enumerate(out_refs):
        base = place_ref[1] ^ step
        for request in range(requests):
            owner = table_ref[base * requests + request] // 2
            out_ref[request * 2 * part_rows : (request + 1) * 2 * part_rows] = incoming_ref[
                owner, 0 : 2 * part_rows
            ]
        drawn = [
            pair_row(table_ref[base * requests + 2 * i], table_ref[base * requests + 2 * i + 1])
            for i in range(requests // 2)
        ]
        notes = jnp.concatenate(
            [row.astype(F32) for row in shared + own + drawn] + [pieces, blank], axis=0
        )
        out_ref[requests * 2 * part_rows :] = notes.astype(BF16)


def gather(place, table, weight, ids, incoming, bases, part_rows, block_total):
    rows = table.shape[0] // bases * 2 * part_rows + NOTE_ROWS
    return pl.pallas_call(
        functools.partial(gather_kernel, part_rows, block_total),
        out_shape=[jax.ShapeDtypeStruct((rows, HEAD_DIM), BF16)] * bases,
        in_specs=[SMEM, SMEM, SMEM, VMEM, VMEM],
        out_specs=[VMEM] * bases,
        cost_estimate=pl.CostEstimate(flops=0, bytes_accessed=1_000_000, transcendentals=0),
        name="gather",
    )(place, table, weight, ids, incoming)


def attention_kernel(
    samples,
    heads,
    part_rows,
    block_total,
    place_ref,
    table_ref,
    refs_ref,
    query_ref,
    key_ref,
    value_ref,
    cot_ref,
    glob_ref,
    below_ref,
    above_ref,
    *refs,
):
    rand_refs = refs[0:samples]
    (
        local_ref,
        glob_term_ref,
        low_rim_ref,
        high_rim_ref,
        rand_term_ref,
        raw_ref,
        term_ref,
        query_term_ref,
        notes_ref,
        bias_ref,
    ) = refs[samples:]
    inv_root = 1.0 / math.sqrt(HEAD_DIM)
    bank = refs_ref.shape[1]
    parts = samples
    slots = 2 * RAND
    seq_rank, base_rank, glob_block = place_ref[0], place_ref[1], place_ref[2]
    rank = lax.broadcasted_iota(jnp.int32, (bank, HEAD_DIM), 0).astype(F32)
    lane = lax.broadcasted_iota(jnp.int32, (BLOCK, HEAD_DIM), 1)
    note_start = rand_refs[0].shape[0] - NOTE_ROWS
    for step in range(samples):
        notes_ref[step] = rand_refs[step][note_start:].astype(F32)
    own_notes = 3
    drawn_notes = 4
    weight_note = drawn_notes + heads * RAND

    def live_blocks(head, index):
        here_block = seq_rank * 2 + index
        listed = [here_block - 1, here_block, here_block + 1, glob_block]
        for slot in range(RAND):
            listed.append(table_ref[((base_rank * heads + head) * 2 + index) * RAND + slot])
        alive = []
        for slot, block in enumerate(listed):
            flag = (block >= 0) & (block < block_total)
            for earlier in listed[:slot]:
                flag = flag & (block != earlier)
            alive.append(jnp.where(flag, 0.0, -1e30))
        dead = jnp.float32(-1e30)
        window = [dead] * index + alive[0:3] + [dead] * (1 - index)
        drawn = [dead] * (index * RAND) + alive[4:] + [dead] * ((1 - index) * RAND)
        return window + [alive[3], dead] + drawn

    cots, queries = [], []
    for head in range(heads):
        cols = columns((base_rank * heads + head) * HEAD_DIM)
        for kv in range(2):
            own = (key_ref, value_ref)[kv]
            to = slice(kv * HEAD_DIM, (kv + 1) * HEAD_DIM)
            unit = slice((head * 2 + kv) * BLOCK, (head * 2 + kv + 1) * BLOCK)
            raw_ref[head, 0:64, to] = below_ref[unit]
            raw_ref[head, 64:192, to] = own[:, cols]
            raw_ref[head, 192:256, to] = above_ref[unit]
            raw_ref[head, 256:320, to] = glob_ref[unit]
            raw_ref[head, 320:384, to] = jnp.zeros((BLOCK, HEAD_DIM), BF16)
        for block, (left, right) in enumerate(zip(live_blocks(head, 0), live_blocks(head, 1))):
            bias_ref[head, block * BLOCK : (block + 1) * BLOCK] = jnp.where(
                lane < BLOCK, left, right
            )
        cots.append(cot_ref[:, cols])
        queries.append(query_ref[:, cols].astype(F32))
    wide = pl.ds(pl.multiple_of(base_rank * heads * HEAD_DIM, heads * HEAD_DIM), heads * HEAD_DIM)
    ref_q = refs_ref[0, :, wide]
    ref_kvs = [
        jnp.concatenate(
            [
                refs_ref[1, :, columns((base_rank * heads + head) * HEAD_DIM)],
                refs_ref[2, :, columns((base_rank * heads + head) * HEAD_DIM)],
            ],
            axis=1,
        )
        for head in range(heads)
    ]
    ref_all = jnp.concatenate(ref_kvs, axis=1)
    for head in range(heads):
        for kv in range(2):
            to = slice(kv * HEAD_DIM, (kv + 1) * HEAD_DIM)
            for slot in range(slots):
                for step in range(parts):
                    start = NEAR + slot * BLOCK + (base_rank ^ step) * part_rows
                    source = ((head * slots + slot) * 2 + kv) * part_rows
                    raw_ref[head, pl.ds(pl.multiple_of(start, part_rows), part_rows), to] = (
                        rand_refs[step][source : source + part_rows]
                    )

    term_ref[...] = jnp.zeros_like(term_ref)
    query_term_ref[...] = jnp.zeros_like(query_term_ref)

    def one_sample(sample, carry):
        notes = notes_ref[sample]

        def hot(row):
            return jnp.where(rank == notes[row : row + 1], 1.0, 0.0).astype(BF16)

        weight = (
            notes[weight_note : weight_note + 1, 0:1]
            + notes[weight_note : weight_note + 1, 1:2]
            + notes[weight_note : weight_note + 1, 2:3]
        )
        hot_near = jnp.concatenate([hot(0), hot(1), hot(2)], axis=1)
        base_near = matmul(hot_near, ref_all, ((0,), (0,)))
        base_rows = matmul(hot(own_notes), ref_q, ((0,), (0,)))
        for head in range(heads):
            here = slice(head * HEAD_DIM, (head + 1) * HEAD_DIM)
            drawn = drawn_notes + head * RAND
            hot_far = jnp.concatenate([hot(drawn), hot(drawn + 1)], axis=1)
            base = jnp.concatenate(
                [
                    base_near[:, head * 2 * HEAD_DIM : (head + 1) * 2 * HEAD_DIM],
                    matmul(hot_far, ref_kvs[head], ((0,), (0,))),
                ],
                axis=0,
            )
            diff = raw_ref[head].astype(F32) - base
            mix = (base + weight * diff).astype(BF16)
            k_mix, v_mix = mix[:, 0:HEAD_DIM], mix[:, HEAD_DIM:]
            base_q = base_rows[:, here]
            diff_q = queries[head] - base_q
            q_mix = (base_q + weight * diff_q).astype(BF16)
            cot = cots[head]
            scores = matmul(k_mix, q_mix, ((1,), (1,))) * inv_root + bias_ref[head]
            exponent = jnp.exp(scores - jnp.max(scores, axis=0, keepdims=True))
            probs = exponent * (1.0 / jnp.sum(exponent, axis=0, keepdims=True))
            probs_low = probs.astype(BF16)
            dprobs = matmul(v_mix, cot, ((1,), (1,)))
            row_term = jnp.sum(probs_low.astype(F32) * dprobs, axis=0, keepdims=True)
            dscore = (probs * (dprobs - row_term)).astype(BF16)
            query_term_ref[head] += diff_q * (matmul(dscore, k_mix, ((0,), (0,))) * inv_root)
            grad_k = matmul(dscore, q_mix, ((1,), (0,)))
            grad_v = matmul(probs_low, cot, ((1,), (0,)))
            term_ref[head] += diff[:, 0:HEAD_DIM] * (grad_k * inv_root) + diff[:, HEAD_DIM:] * grad_v
        return carry

    lax.fori_loop(0, samples, one_sample, 0)
    for head in range(heads):
        here = slice(head * HEAD_DIM, (head + 1) * HEAD_DIM)
        local_ref[:, here] = term_ref[head, 64:192] + query_term_ref[head]
    for head in range(heads):
        here = slice(head * HEAD_DIM, (head + 1) * HEAD_DIM)
        low_rim_ref[:, here] = term_ref[head, 0:64].astype(BF16)
        high_rim_ref[:, here] = term_ref[head, 192:256].astype(BF16)
        glob_term_ref[head * BLOCK : (head + 1) * BLOCK] = term_ref[head, 256:320].astype(BF16)
        for slot in range(slots):
            for part in range(parts):
                start = NEAR + slot * BLOCK + part * part_rows
                rand_term_ref[part, head * slots + slot] = term_ref[
                    head, start : start + part_rows
                ].astype(BF16)


def attention(
    place, table, refs, query, key, value, cot, glob, below, above, rand, part_rows, heads, block_total
):
    samples = len(rand)
    slots = heads * 2 * RAND
    feat = heads * HEAD_DIM
    return pl.pallas_call(
        functools.partial(attention_kernel, samples, heads, part_rows, block_total),
        out_shape=[
            jax.ShapeDtypeStruct((2 * BLOCK, feat), F32),
            jax.ShapeDtypeStruct((heads * BLOCK, HEAD_DIM), BF16),
            jax.ShapeDtypeStruct((BLOCK, feat), BF16),
            jax.ShapeDtypeStruct((BLOCK, feat), BF16),
            jax.ShapeDtypeStruct((samples, slots, part_rows, HEAD_DIM), BF16),
        ],
        in_specs=[SMEM, SMEM] + [VMEM] * (8 + samples),
        out_specs=[VMEM] * 5,
        scratch_shapes=[
            pltpu.VMEM((heads, 10 * BLOCK, 2 * HEAD_DIM), BF16),
            pltpu.VMEM((heads, 10 * BLOCK, HEAD_DIM), F32),
            pltpu.VMEM((heads, 2 * BLOCK, HEAD_DIM), F32),
            pltpu.VMEM((samples, NOTE_ROWS, HEAD_DIM), F32),
            pltpu.VMEM((heads, 10 * BLOCK, HEAD_DIM), F32),
        ],
        compiler_params=pltpu.CompilerParams(vmem_limit_bytes=32 * 1024 * 1024),
        cost_estimate=pl.CostEstimate(
            flops=900_000_000, bytes_accessed=2_000_000, transcendentals=600_000
        ),
        name="attention",
    )(place, table, refs, query, key, value, cot, glob, below, above, *rand)


def collect_kernel(heads, place_ref, pick_ref, arrived_ref, *refs):
    out_refs, sum_ref, total_ref = refs[0:-2], refs[-2], refs[-1]
    bases = len(out_refs)
    part_rows = total_ref.shape[1]
    head_count = heads * bases
    total_ref[...] = jnp.zeros_like(total_ref)

    def one_slot(slot, glob):
        unit = pick_ref[slot]
        total_ref[unit] += arrived_ref[slot, 0:part_rows].astype(F32)
        return glob + arrived_ref[slot, part_rows:].astype(F32)

    rows = arrived_ref.shape[1] - part_rows
    glob = lax.fori_loop(
        0, pick_ref.shape[0], one_slot, jnp.zeros((rows, HEAD_DIM), F32), unroll=8
    )
    for copy in range(sum_ref.shape[0]):
        sum_ref[copy] = glob.astype(BF16)
    for step, out_ref in enumerate(out_refs):
        base = place_ref[1] ^ step
        for block in range(2):
            for head in range(heads):
                out_ref[block * heads + head] = total_ref[
                    1 + block * head_count + base * heads + head
                ].astype(BF16)


def collect(place, pick, arrived, bases, part_rows, heads, copies):
    rows = arrived.shape[1] - part_rows
    return pl.pallas_call(
        functools.partial(collect_kernel, heads),
        out_shape=[jax.ShapeDtypeStruct((2 * heads, part_rows, HEAD_DIM), BF16)] * bases
        + [jax.ShapeDtypeStruct((copies, rows, HEAD_DIM), BF16)],
        in_specs=[SMEM, SMEM, VMEM],
        out_specs=[VMEM] * (bases + 1),
        scratch_shapes=[pltpu.VMEM((1 + 2 * heads * bases, part_rows, HEAD_DIM), F32)],
        cost_estimate=pl.CostEstimate(flops=0, bytes_accessed=500_000, transcendentals=0),
        name="collect",
    )(place, pick, arrived)


def finish_kernel(heads, place_ref, local_ref, low_ref, high_ref, glob_ref, *refs):
    back_refs, out_ref, total_ref = refs[0:-2], refs[-2], refs[-1]
    bases = len(back_refs)
    part_rows = back_refs[0].shape[1]
    total_ref[0:BLOCK] = local_ref[0:BLOCK] + low_ref[...].astype(F32)
    total_ref[BLOCK:] = local_ref[BLOCK:] + high_ref[...].astype(F32)
    for head in range(heads):
        here = slice(head * HEAD_DIM, (head + 1) * HEAD_DIM)
        for step, back_ref in enumerate(back_refs):
            for block in range(2):
                start = block * BLOCK + (place_ref[1] ^ step) * part_rows
                rows = pl.ds(pl.multiple_of(start, part_rows), part_rows)
                total_ref[rows, here] += back_ref[block * heads + head].astype(F32)
        glob = glob_ref[head * BLOCK : (head + 1) * BLOCK].astype(F32)
        for block in range(2):
            rows = slice(block * BLOCK, (block + 1) * BLOCK)
            mine = place_ref[0] * 2 + block == place_ref[2]
            total_ref[rows, here] += jnp.where(mine, glob, 0.0)
    out_ref[...] = (total_ref[...] * (1.0 / bases)).astype(BF16)


def finish(place, local, low, high, glob, back, heads):
    return pl.pallas_call(
        functools.partial(finish_kernel, heads),
        out_shape=jax.ShapeDtypeStruct(local.shape, BF16),
        in_specs=[SMEM] + [VMEM] * (4 + len(back)),
        out_specs=VMEM,
        scratch_shapes=[pltpu.VMEM(local.shape, F32)],
        cost_estimate=pl.CostEstimate(flops=0, bytes_accessed=400_000, transcendentals=0),
        name="finish",
    )(place, local, low, high, glob, *back)


def exchange(array, axis, groups=None):
    return lax.all_to_all(array, axis, 0, 0, axis_index_groups=groups, tiled=True)


def swapped(arrays):
    return [arrays[0]] + [
        lax.ppermute(arrays[step], "base", [(i, i ^ step) for i in range(len(arrays))])
        for step in range(1, len(arrays))
    ]


def runs(count, size):
    return [list(range(i, i + size)) for i in range(0, count, size)]


def take(array, index):
    return array.at[index].get(mode="promise_in_bounds")


def per_device(
    queries,
    key_rows,
    values,
    cotangent,
    reference_set,
    sample_ids,
    mix_weight,
    global_block,
    random_blocks,
):
    seq_count = lax.axis_size("seq")
    seq_rank = lax.axis_index("seq")
    base_count = lax.axis_size("base")
    base_rank = lax.axis_index("base")
    tok_dev, feat_dev = queries.shape
    per_dev = tok_dev // BLOCK
    head_count = feat_dev // HEAD_DIM
    heads = head_count // base_count
    feat = heads * HEAD_DIM
    block_total = per_dev * seq_count
    requests = head_count * per_dev * RAND
    part_rows = BLOCK // base_count
    global_id = global_block[0]
    owner_glob = global_id // per_dev
    place = jnp.stack([seq_rank, base_rank, global_id]).astype(jnp.int32)

    table = random_blocks.reshape(head_count, seq_count, per_dev, RAND)
    unit = (table % per_dev) * head_count + jnp.arange(head_count)[:, None, None, None]
    wanted = table // per_dev == seq_rank
    pick = jnp.sum(jnp.where(wanted, unit + 1, 0), axis=(0, 2, 3))
    my_table = lax.dynamic_index_in_dim(table, seq_rank, 1, keepdims=False).reshape(requests)
    my_owner = my_table // per_dev

    outgoing, low, high = prepare(global_block, pick, key_rows, values, part_rows, heads)

    up = [(i, (i + 1) % seq_count) for i in range(seq_count)]
    down = [((i + 1) % seq_count, i) for i in range(seq_count)]
    below = lax.ppermute(high, "seq", up)
    above = lax.ppermute(low, "seq", down)

    incoming = exchange(outgoing, "seq")
    piece = lax.dynamic_index_in_dim(incoming, owner_glob, 0, keepdims=False)[2 * part_rows :]
    ways = low.shape[0] // PIECE
    glob = exchange(
        jnp.broadcast_to(piece[None], (ways,) + piece.shape), "seq", runs(seq_count, ways)
    ).reshape(low.shape)
    ids = sample_ids.reshape(-1, HEAD_DIM)
    rand = swapped(
        gather(place, my_table, mix_weight, ids, incoming, base_count, part_rows, block_total)
    )

    local, glob_term, low_rim, high_rim, rand_term = attention(
        place,
        my_table,
        reference_set,
        queries,
        key_rows,
        values,
        cotangent,
        glob,
        below,
        above,
        rand,
        part_rows,
        heads,
        block_total,
    )

    from_above = lax.ppermute(low_rim, "seq", down)
    from_below = lax.ppermute(high_rim, "seq", up)

    terms = exchange(rand_term.reshape(-1, part_rows, HEAD_DIM), "base")
    order = jnp.arange(1, requests + 1)
    sent = jnp.sum(
        jnp.where(my_owner[None, :] == jnp.arange(seq_count)[:, None], order[None, :], 0), axis=1
    )
    shares = jnp.tile(
        glob_term.reshape(SHARES, -1, HEAD_DIM), (seq_count // SHARES, 1, 1)
    )
    returning = jnp.concatenate([take(terms, jnp.maximum(sent - 1, 0)), shares], axis=1)
    arrived = exchange(returning, "seq")
    arrived, from_below, from_above = lax.optimization_barrier((arrived, from_below, from_above))
    *back, share = collect(place, pick, arrived, base_count, part_rows, heads, SHARES)
    back = swapped(back)
    glob_total = exchange(share, "seq", runs(seq_count, SHARES)).reshape(glob_term.shape)
    return finish(place, local, from_below, from_above, glob_total, back, heads)


def solution(mesh):
    placed = (
        P("seq", "head"),
        P("seq", "head"),
        P("seq", "head"),
        P("seq", "head"),
        P(None, None, "head"),
        P("base", None),
        P("base"),
        P(),
        P("head", None, None),
    )
    return jax.shard_map(
        per_device,
        mesh=mesh,
        in_specs=placed,
        out_specs=P("seq", ("head", "base")),
        check_vma=False,
    )
```

```python
import functools
import math

import jax
import jax.numpy as jnp
from jax import lax
from jax.experimental import pallas as pl
from jax.experimental.pallas import tpu as pltpu
from jax.sharding import PartitionSpec as P

HEAD_DIM = 128
BLOCK = 64
RAND = 2
SHARES = 16
PIECE = 8
NOTE_ROWS = 16
NEAR = 6 * BLOCK
BF16 = jnp.bfloat16
F32 = jnp.float32
VMEM = pl.BlockSpec(memory_space=pltpu.VMEM)
SMEM = pl.BlockSpec(memory_space=pltpu.SMEM)


def matmul(left, right, dims):
    return lax.dot_general(left, right, (dims, ((), ())), preferred_element_type=F32)


def columns(first):
    return pl.ds(pl.multiple_of(first, HEAD_DIM), HEAD_DIM)


def prepare_kernel(
    part_rows, heads, glob_ref, pick_ref, key_ref, value_ref, outgoing_ref, low_ref, high_ref
):
    base_rank = lax.axis_index("base")
    head_count = key_ref.shape[1] // HEAD_DIM
    glob_start = pl.multiple_of((glob_ref[0] % 2) * BLOCK, BLOCK)

    def one_slot(slot, carry):
        unit = jnp.maximum(pick_ref[slot] - 1, 0)
        rows = pl.ds(
            pl.multiple_of((unit // head_count) * BLOCK + base_rank * part_rows, part_rows),
            part_rows,
        )
        cols = columns((unit % head_count) * HEAD_DIM)
        outgoing_ref[slot, 0:part_rows] = key_ref[rows, cols]
        outgoing_ref[slot, part_rows : 2 * part_rows] = value_ref[rows, cols]
        return carry

    lax.fori_loop(0, pick_ref.shape[0], one_slot, 0, unroll=8)
    pieces = heads * 2 * BLOCK // PIECE
    for head in range(heads):
        cols = columns((base_rank * heads + head) * HEAD_DIM)
        for kv in range(2):
            own = (key_ref, value_ref)[kv]
            unit = slice((head * 2 + kv) * BLOCK, (head * 2 + kv + 1) * BLOCK)
            low_ref[unit] = own[0:BLOCK, cols]
            high_ref[unit] = own[BLOCK:, cols]
            rows = own[pl.ds(glob_start, BLOCK), cols].astype(F32)
            for i in range(BLOCK // PIECE):
                piece = rows[i * PIECE : (i + 1) * PIECE].astype(BF16)
                first = (head * 2 + kv) * (BLOCK // PIECE) + i
                for slot in range(first, pick_ref.shape[0], pieces):
                    outgoing_ref[slot, 2 * part_rows :] = piece


def prepare(glob_block, pick, key_rows, value_rows, part_rows, heads):
    edge = jax.ShapeDtypeStruct((heads * 2 * BLOCK, HEAD_DIM), BF16)
    return pl.pallas_call(
        functools.partial(prepare_kernel, part_rows, heads),
        out_shape=[
            jax.ShapeDtypeStruct((pick.shape[0], 2 * part_rows + PIECE, HEAD_DIM), BF16),
            edge,
            edge,
        ],
        in_specs=[SMEM, SMEM, VMEM, VMEM],
        out_specs=[VMEM] * 3,
        cost_estimate=pl.CostEstimate(flops=0, bytes_accessed=1_400_000, transcendentals=0),
        name="prepare",
    )(glob_block, pick, key_rows, value_rows)


def gather_kernel(
    steps,
    requests,
    part_rows,
    block_total,
    glob_ref,
    table_ref,
    weight_ref,
    ids_ref,
    incoming_ref,
    *out_refs,
):
    lane = lax.broadcasted_iota(jnp.int32, (1, HEAD_DIM), 1)

    def block_row(block, half):
        row = ids_ref[pl.ds(block // 2, 1), :]
        return jnp.where(block % 2 == half, row, pltpu.roll(row, BLOCK, 1))

    def pair_row(left, right):
        return jnp.where(lane < BLOCK, block_row(left, 0), block_row(right, 1))

    first = lax.axis_index("seq") * 2
    glob = glob_ref[0]
    below = jnp.maximum(first - 1, 0)
    above = jnp.minimum(first + 2, block_total - 1)
    shared = [pair_row(below, first), pair_row(first + 1, above), pair_row(glob, glob)]
    own = [pair_row(first, first + 1)]
    weight = jnp.full((1, HEAD_DIM), weight_ref[0], F32)
    high = weight.astype(BF16).astype(F32)
    rest = weight - high
    middle = rest.astype(BF16).astype(F32)
    pieces = jnp.where(lane == 0, high, jnp.where(lane == 1, middle, rest - middle))
    blank = jnp.zeros((NOTE_ROWS - 5 - requests // 2, HEAD_DIM), F32)
    for step, out_ref in zip(steps, out_refs):
        base = lax.axis_index("base") ^ step
        for request in range(requests):
            owner = table_ref[base * requests + request] // 2
            out_ref[request * 2 * part_rows : (request + 1) * 2 * part_rows] = incoming_ref[
                owner, 0 : 2 * part_rows
            ]
        drawn = [
            pair_row(table_ref[base * requests + 2 * i], table_ref[base * requests + 2 * i + 1])
            for i in range(requests // 2)
        ]
        notes = jnp.concatenate(
            [row.astype(F32) for row in shared + own + drawn] + [pieces, blank], axis=0
        )
        out_ref[requests * 2 * part_rows :] = notes.astype(BF16)


def gather(glob_block, table, weight, ids, incoming, steps, bases, part_rows, block_total):
    requests = table.shape[0] // bases
    rows = requests * 2 * part_rows + NOTE_ROWS
    return pl.pallas_call(
        functools.partial(gather_kernel, steps, requests, part_rows, block_total),
        out_shape=[jax.ShapeDtypeStruct((rows, HEAD_DIM), BF16)] * len(steps),
        in_specs=[SMEM, SMEM, SMEM, VMEM, VMEM],
        out_specs=[VMEM] * len(steps),
        cost_estimate=pl.CostEstimate(flops=0, bytes_accessed=1_000_000, transcendentals=0),
        name="gather",
    )(glob_block, table, weight, ids, incoming)


def attention_kernel(
    samples,
    heads,
    part_rows,
    block_total,
    place_ref,
    table_ref,
    refs_ref,
    query_ref,
    key_ref,
    value_ref,
    cot_ref,
    glob_ref,
    below_ref,
    above_ref,
    *refs,
):
    rand_refs = refs[0:samples]
    (
        local_ref,
        glob_term_ref,
        low_rim_ref,
        high_rim_ref,
        rand_term_ref,
        raw_ref,
        term_ref,
        query_term_ref,
        notes_ref,
        bias_ref,
    ) = refs[samples:]
    inv_root = 1.0 / math.sqrt(HEAD_DIM)
    bank = refs_ref.shape[1]
    parts = samples
    slots = 2 * RAND
    seq_rank, base_rank, glob_block = place_ref[0], place_ref[1], place_ref[2]
    rank = lax.broadcasted_iota(jnp.int32, (bank, HEAD_DIM), 0).astype(F32)
    lane = lax.broadcasted_iota(jnp.int32, (BLOCK, HEAD_DIM), 1)
    note_start = rand_refs[0].shape[0] - NOTE_ROWS
    for step in range(samples):
        notes_ref[step] = rand_refs[step][note_start:].astype(F32)
    own_notes = 3
    drawn_notes = 4
    weight_note = drawn_notes + heads * RAND

    def live_blocks(head, index):
        here_block = seq_rank * 2 + index
        listed = [here_block - 1, here_block, here_block + 1, glob_block]
        for slot in range(RAND):
            listed.append(table_ref[((base_rank * heads + head) * 2 + index) * RAND + slot])
        alive = []
        for slot, block in enumerate(listed):
            flag = (block >= 0) & (block < block_total)
            for earlier in listed[:slot]:
                flag = flag & (block != earlier)
            alive.append(jnp.where(flag, 0.0, -1e30))
        dead = jnp.float32(-1e30)
        window = [dead] * index + alive[0:3] + [dead] * (1 - index)
        drawn = [dead] * (index * RAND) + alive[4:] + [dead] * ((1 - index) * RAND)
        return window + [alive[3], dead] + drawn

    cots, queries = [], []
    for head in range(heads):
        cols = columns((base_rank * heads + head) * HEAD_DIM)
        for kv in range(2):
            own = (key_ref, value_ref)[kv]
            to = slice(kv * HEAD_DIM, (kv + 1) * HEAD_DIM)
            unit = slice((head * 2 + kv) * BLOCK, (head * 2 + kv + 1) * BLOCK)
            raw_ref[head, 0:64, to] = below_ref[unit]
            raw_ref[head, 64:192, to] = own[:, cols]
            raw_ref[head, 192:256, to] = above_ref[unit]
            raw_ref[head, 256:320, to] = glob_ref[unit]
            raw_ref[head, 320:384, to] = jnp.zeros((BLOCK, HEAD_DIM), BF16)
        for block, (left, right) in enumerate(zip(live_blocks(head, 0), live_blocks(head, 1))):
            bias_ref[head, block * BLOCK : (block + 1) * BLOCK] = jnp.where(
                lane < BLOCK, left, right
            )
        cots.append(cot_ref[:, cols])
        queries.append(query_ref[:, cols].astype(F32))
    wide = pl.ds(pl.multiple_of(base_rank * heads * HEAD_DIM, heads * HEAD_DIM), heads * HEAD_DIM)
    ref_q = refs_ref[0, :, wide]
    ref_kvs = [
        jnp.concatenate(
            [
                refs_ref[1, :, columns((base_rank * heads + head) * HEAD_DIM)],
                refs_ref[2, :, columns((base_rank * heads + head) * HEAD_DIM)],
            ],
            axis=1,
        )
        for head in range(heads)
    ]
    ref_all = jnp.concatenate(ref_kvs, axis=1)
    for head in range(heads):
        for kv in range(2):
            to = slice(kv * HEAD_DIM, (kv + 1) * HEAD_DIM)
            for slot in range(slots):
                for step in range(parts):
                    start = NEAR + slot * BLOCK + (base_rank ^ step) * part_rows
                    source = ((head * slots + slot) * 2 + kv) * part_rows
                    raw_ref[head, pl.ds(pl.multiple_of(start, part_rows), part_rows), to] = (
                        rand_refs[step][source : source + part_rows]
                    )

    term_ref[...] = jnp.zeros_like(term_ref)
    query_term_ref[...] = jnp.zeros_like(query_term_ref)

    def one_sample(sample, carry):
        notes = notes_ref[sample]

        def hot(row):
            return jnp.where(rank == notes[row : row + 1], 1.0, 0.0).astype(BF16)

        weight = (
            notes[weight_note : weight_note + 1, 0:1]
            + notes[weight_note : weight_note + 1, 1:2]
            + notes[weight_note : weight_note + 1, 2:3]
        )
        hot_near = jnp.concatenate([hot(0), hot(1), hot(2)], axis=1)
        base_near = matmul(hot_near, ref_all, ((0,), (0,)))
        base_rows = matmul(hot(own_notes), ref_q, ((0,), (0,)))
        for head in range(heads):
            here = slice(head * HEAD_DIM, (head + 1) * HEAD_DIM)
            drawn = drawn_notes + head * RAND
            hot_far = jnp.concatenate([hot(drawn), hot(drawn + 1)], axis=1)
            base = jnp.concatenate(
                [
                    base_near[:, head * 2 * HEAD_DIM : (head + 1) * 2 * HEAD_DIM],
                    matmul(hot_far, ref_kvs[head], ((0,), (0,))),
                ],
                axis=0,
            )
            diff = raw_ref[head].astype(F32) - base
            mix = (base + weight * diff).astype(BF16)
            k_mix, v_mix = mix[:, 0:HEAD_DIM], mix[:, HEAD_DIM:]
            base_q = base_rows[:, here]
            diff_q = queries[head] - base_q
            q_mix = (base_q + weight * diff_q).astype(BF16)
            cot = cots[head]
            scores = matmul(k_mix, q_mix, ((1,), (1,))) * inv_root + bias_ref[head]
            exponent = jnp.exp(scores - jnp.max(scores, axis=0, keepdims=True))
            probs = exponent * (1.0 / jnp.sum(exponent, axis=0, keepdims=True))
            probs_low = probs.astype(BF16)
            dprobs = matmul(v_mix, cot, ((1,), (1,)))
            row_term = jnp.sum(probs_low.astype(F32) * dprobs, axis=0, keepdims=True)
            dscore = (probs * (dprobs - row_term)).astype(BF16)
            query_term_ref[head] += diff_q * (matmul(dscore, k_mix, ((0,), (0,))) * inv_root)
            grad_k = matmul(dscore, q_mix, ((1,), (0,)))
            grad_v = matmul(probs_low, cot, ((1,), (0,)))
            term_ref[head] += diff[:, 0:HEAD_DIM] * (grad_k * inv_root) + diff[:, HEAD_DIM:] * grad_v
        return carry

    lax.fori_loop(0, samples, one_sample, 0)
    for head in range(heads):
        here = slice(head * HEAD_DIM, (head + 1) * HEAD_DIM)
        local_ref[:, here] = term_ref[head, 64:192] + query_term_ref[head]
    for head in range(heads):
        here = slice(head * HEAD_DIM, (head + 1) * HEAD_DIM)
        low_rim_ref[:, here] = term_ref[head, 0:64].astype(BF16)
        high_rim_ref[:, here] = term_ref[head, 192:256].astype(BF16)
        glob_term_ref[head * BLOCK : (head + 1) * BLOCK] = term_ref[head, 256:320].astype(BF16)
        for slot in range(slots):
            for part in range(parts):
                start = NEAR + slot * BLOCK + part * part_rows
                rand_term_ref[part, head * slots + slot] = term_ref[
                    head, start : start + part_rows
                ].astype(BF16)


def attention(
    place, table, refs, query, key, value, cot, glob, below, above, rand, part_rows, heads, block_total
):
    samples = len(rand)
    slots = heads * 2 * RAND
    feat = heads * HEAD_DIM
    return pl.pallas_call(
        functools.partial(attention_kernel, samples, heads, part_rows, block_total),
        out_shape=[
            jax.ShapeDtypeStruct((2 * BLOCK, feat), F32),
            jax.ShapeDtypeStruct((heads * BLOCK, HEAD_DIM), BF16),
            jax.ShapeDtypeStruct((BLOCK, feat), BF16),
            jax.ShapeDtypeStruct((BLOCK, feat), BF16),
            jax.ShapeDtypeStruct((samples, slots, part_rows, HEAD_DIM), BF16),
        ],
        in_specs=[SMEM, SMEM] + [VMEM] * (8 + samples),
        out_specs=[VMEM] * 5,
        scratch_shapes=[
            pltpu.VMEM((heads, 10 * BLOCK, 2 * HEAD_DIM), BF16),
            pltpu.VMEM((heads, 10 * BLOCK, HEAD_DIM), F32),
            pltpu.VMEM((heads, 2 * BLOCK, HEAD_DIM), F32),
            pltpu.VMEM((samples, NOTE_ROWS, HEAD_DIM), F32),
            pltpu.VMEM((heads, 10 * BLOCK, HEAD_DIM), F32),
        ],
        compiler_params=pltpu.CompilerParams(vmem_limit_bytes=32 * 1024 * 1024),
        cost_estimate=pl.CostEstimate(
            flops=900_000_000, bytes_accessed=2_000_000, transcendentals=600_000
        ),
        name="attention",
    )(place, table, refs, query, key, value, cot, glob, below, above, *rand)


def collect_kernel(heads, place_ref, pick_ref, arrived_ref, *refs):
    out_refs, sum_ref, total_ref = refs[0:-2], refs[-2], refs[-1]
    bases = len(out_refs)
    part_rows = total_ref.shape[1]
    head_count = heads * bases
    total_ref[...] = jnp.zeros_like(total_ref)

    def one_slot(slot, glob):
        unit = pick_ref[slot]
        total_ref[unit] += arrived_ref[slot, 0:part_rows].astype(F32)
        return glob + arrived_ref[slot, part_rows:].astype(F32)

    rows = arrived_ref.shape[1] - part_rows
    glob = lax.fori_loop(
        0, pick_ref.shape[0], one_slot, jnp.zeros((rows, HEAD_DIM), F32), unroll=8
    )
    for copy in range(sum_ref.shape[0]):
        sum_ref[copy] = glob.astype(BF16)
    for step, out_ref in enumerate(out_refs):
        base = place_ref[1] ^ step
        for block in range(2):
            for head in range(heads):
                out_ref[block * heads + head] = total_ref[
                    1 + block * head_count + base * heads + head
                ].astype(BF16)


def collect(place, pick, arrived, bases, part_rows, heads, copies):
    rows = arrived.shape[1] - part_rows
    return pl.pallas_call(
        functools.partial(collect_kernel, heads),
        out_shape=[jax.ShapeDtypeStruct((2 * heads, part_rows, HEAD_DIM), BF16)] * bases
        + [jax.ShapeDtypeStruct((copies, rows, HEAD_DIM), BF16)],
        in_specs=[SMEM, SMEM, VMEM],
        out_specs=[VMEM] * (bases + 1),
        scratch_shapes=[pltpu.VMEM((1 + 2 * heads * bases, part_rows, HEAD_DIM), F32)],
        cost_estimate=pl.CostEstimate(flops=0, bytes_accessed=500_000, transcendentals=0),
        name="collect",
    )(place, pick, arrived)


def finish_kernel(heads, place_ref, local_ref, low_ref, high_ref, glob_ref, *refs):
    back_refs, out_ref, total_ref = refs[0:-2], refs[-2], refs[-1]
    bases = len(back_refs)
    part_rows = back_refs[0].shape[1]
    total_ref[0:BLOCK] = local_ref[0:BLOCK] + low_ref[...].astype(F32)
    total_ref[BLOCK:] = local_ref[BLOCK:] + high_ref[...].astype(F32)
    for head in range(heads):
        here = slice(head * HEAD_DIM, (head + 1) * HEAD_DIM)
        for step, back_ref in enumerate(back_refs):
            for block in range(2):
                start = block * BLOCK + (place_ref[1] ^ step) * part_rows
                rows = pl.ds(pl.multiple_of(start, part_rows), part_rows)
                total_ref[rows, here] += back_ref[block * heads + head].astype(F32)
        glob = glob_ref[head * BLOCK : (head + 1) * BLOCK].astype(F32)
        for block in range(2):
            rows = slice(block * BLOCK, (block + 1) * BLOCK)
            mine = place_ref[0] * 2 + block == place_ref[2]
            total_ref[rows, here] += jnp.where(mine, glob, 0.0)
    out_ref[...] = (total_ref[...] * (1.0 / bases)).astype(BF16)


def finish(place, local, low, high, glob, back, heads):
    return pl.pallas_call(
        functools.partial(finish_kernel, heads),
        out_shape=jax.ShapeDtypeStruct(local.shape, BF16),
        in_specs=[SMEM] + [VMEM] * (4 + len(back)),
        out_specs=VMEM,
        scratch_shapes=[pltpu.VMEM(local.shape, F32)],
        cost_estimate=pl.CostEstimate(flops=0, bytes_accessed=400_000, transcendentals=0),
        name="finish",
    )(place, local, low, high, glob, *back)


def exchange(array, axis, groups=None):
    return lax.all_to_all(array, axis, 0, 0, axis_index_groups=groups, tiled=True)


def swapped(arrays):
    return [arrays[0]] + [
        lax.ppermute(arrays[step], "base", [(i, i ^ step) for i in range(len(arrays))])
        for step in range(1, len(arrays))
    ]


def runs(count, size):
    return [list(range(i, i + size)) for i in range(0, count, size)]


def take(array, index):
    return array.at[index].get(mode="promise_in_bounds")


def per_device(
    queries,
    key_rows,
    values,
    cotangent,
    reference_set,
    sample_ids,
    mix_weight,
    global_block,
    random_blocks,
):
    seq_count = lax.axis_size("seq")
    seq_rank = lax.axis_index("seq")
    base_count = lax.axis_size("base")
    base_rank = lax.axis_index("base")
    tok_dev, feat_dev = queries.shape
    per_dev = tok_dev // BLOCK
    head_count = feat_dev // HEAD_DIM
    heads = head_count // base_count
    feat = heads * HEAD_DIM
    block_total = per_dev * seq_count
    requests = head_count * per_dev * RAND
    part_rows = BLOCK // base_count
    global_id = global_block[0]
    owner_glob = global_id // per_dev
    place = jnp.stack([seq_rank, base_rank, global_id]).astype(jnp.int32)

    table = random_blocks.reshape(head_count, seq_count, per_dev, RAND)
    unit = (table % per_dev) * head_count + jnp.arange(head_count)[:, None, None, None]
    wanted = table // per_dev == seq_rank
    pick = jnp.sum(jnp.where(wanted, unit + 1, 0), axis=(0, 2, 3))
    my_table = lax.dynamic_index_in_dim(table, seq_rank, 1, keepdims=False).reshape(requests)
    my_owner = my_table // per_dev

    outgoing, low, high = prepare(global_block, pick, key_rows, values, part_rows, heads)

    up = [(i, (i + 1) % seq_count) for i in range(seq_count)]
    down = [((i + 1) % seq_count, i) for i in range(seq_count)]
    below = lax.ppermute(high, "seq", up)
    above = lax.ppermute(low, "seq", down)

    incoming = exchange(outgoing, "seq")
    piece = lax.dynamic_index_in_dim(incoming, owner_glob, 0, keepdims=False)[2 * part_rows :]
    ways = low.shape[0] // PIECE
    glob = exchange(
        jnp.broadcast_to(piece[None], (ways,) + piece.shape), "seq", runs(seq_count, ways)
    ).reshape(low.shape)
    ids = sample_ids.reshape(-1, HEAD_DIM)
    sources = (global_block, my_table, mix_weight, ids, incoming)
    sizes = (base_count, part_rows, block_total)
    others = gather(*sources, range(1, base_count), *sizes)
    rand = swapped(gather(*sources, range(1), *sizes) + others)

    local, glob_term, low_rim, high_rim, rand_term = attention(
        place,
        my_table,
        reference_set,
        queries,
        key_rows,
        values,
        cotangent,
        glob,
        below,
        above,
        rand,
        part_rows,
        heads,
        block_total,
    )

    from_above = lax.ppermute(low_rim, "seq", down)
    from_below = lax.ppermute(high_rim, "seq", up)

    terms = exchange(rand_term.reshape(-1, part_rows, HEAD_DIM), "base")
    order = jnp.arange(1, requests + 1)
    sent = jnp.sum(
        jnp.where(my_owner[None, :] == jnp.arange(seq_count)[:, None], order[None, :], 0), axis=1
    )
    shares = jnp.tile(
        glob_term.reshape(SHARES, -1, HEAD_DIM), (seq_count // SHARES, 1, 1)
    )
    returning = jnp.concatenate([take(terms, jnp.maximum(sent - 1, 0)), shares], axis=1)
    arrived = exchange(returning, "seq")
    arrived, from_below, from_above = lax.optimization_barrier((arrived, from_below, from_above))
    *back, share = collect(place, pick, arrived, base_count, part_rows, heads, SHARES)
    back = swapped(back)
    glob_total = exchange(share, "seq", runs(seq_count, SHARES)).reshape(glob_term.shape)
    return finish(place, local, from_below, from_above, glob_total, back, heads)


def solution(mesh):
    placed = (
        P("seq", "head"),
        P("seq", "head"),
        P("seq", "head"),
        P("seq", "head"),
        P(None, None, "head"),
        P("base", None),
        P("base"),
        P(),
        P("head", None, None),
    )
    return jax.shard_map(
        per_device,
        mesh=mesh,
        in_specs=placed,
        out_specs=P("seq", ("head", "base")),
        check_vma=False,
    )
```
